32 devices in a mesh: seq: 16 (over z, y, x), batch: 2 (over core).
Axes of the slice: x: 2, y: 2, z: 4, core: 2. Of those that a mesh axis runs over, the one named last changes fastest.
Arguments:
- inputs: bfloat16 [2, 2048, 256], P('batch', 'seq'), may hold values from -6 to 6
- cotangent: bfloat16 [2, 2048, 256], P('batch', 'seq'), may hold values from -6 to 6
- decay_rate: float32 [32, 256], replicated, as said below
- rotation: float32 [32, 256], replicated, may hold values from -3.140625 to 3.140625
- readout: float32 [2, 32, 256], replicated, may hold values from -1.5 to 1.5
- skip_gain: float32 [256], replicated, may hold values from -4 to 4
- projection: bfloat16 [256, 256], replicated, may hold values from -0.375 to 0.375
Outputs:
- outputs: bfloat16 [2, 2048, 256], P('batch', 'seq')
- input_grad: bfloat16 [2, 2048, 256], P('batch', 'seq')
- proj_grad: float32 [256, 256], replicated
- readout_grad: float32 [2, 32, 256], replicated
- skip_grad: float32 [256], replicated
The draws below stay inside these ranges and needn't reach their ends.
Inputs may be any that keep to these rules, and one draw needn't show every extreme that they name: `decay_rate`: every decay rate is positive.
All inputs are finite; a program needn't handle non-finite values.
Results may differ from the reference program's by a relative error of at most 0.004.
Values sent between devices are 32-bit elements; how exact they have to be, the bound alone decides.
No kernel may reach another device: no remote copies, remote signals or barrier semaphores. Data moves between devices by JAX's collectives and lax.ppermute only.
A program may use at most 128 MiB of HBM per device.

```python
import math
from functools import partial
import jax
import jax.numpy as jnp
from jax import lax

H = 256
N = 32
BLOCK = 16
SEQLEN = 2048
CLIPS = 2


def draw_decay_rate(key, part):
    key_mix, key_slow, key_fast = jax.random.split(key, 3)
    slow_share = 0.5
    slow_mask = jax.random.uniform(key_mix, (N, H)) < slow_share
    slow_rate = jnp.exp(jax.random.uniform(key_slow, (N, H), minval=math.log(0.02 / SEQLEN), maxval=math.log(2.0 / SEQLEN)))
    fast_rate = jnp.exp(jax.random.uniform(key_fast, (N, H), minval=math.log(0.02), maxval=math.log(0.099)))
    return jnp.where(slow_mask, slow_rate, fast_rate).astype(jnp.float32)


def levels(stream_key, extent, cuts, smallest, top_value):
    def one(dim, blocks):
        steps = jax.random.uniform(jax.random.fold_in(jax.random.fold_in(stream_key, 6), dim), (blocks,), jnp.float32, smallest / len(cuts), top_value / len(cuts))
        return jnp.repeat(jnp.exp(steps), extent[dim] // blocks).reshape((-1,) + (1,) * (len(extent) - dim - 1))

    factor_of = one(*cuts[0])
    for cut in cuts[1:]:
        factor_of = factor_of * one(*cut)
    return factor_of


def gaussian(key, extent, deviation, most, shards=(), kind=jnp.bfloat16):
    entries = deviation * jax.random.normal(key, extent, jnp.float32)
    if shards:
        entries = entries * levels(key, extent, shards, -0.22, 0.18)
    return jnp.clip(entries, -most, most).astype(kind)


def setup_inputs(seed: int = 0) -> dict:
    key_list = jax.random.split(jax.random.key(seed), 8)
    return {
        "inputs": gaussian(key_list[0], (CLIPS, SEQLEN, H), 1.0, 6.0, ((0, 2), (1, 16))),
        "cotangent": gaussian(key_list[1], (CLIPS, SEQLEN, H), 1.0, 6.0, ((0, 2), (1, 16))),
        "decay_rate": draw_decay_rate(jax.random.fold_in(key_list[7], 71), 0),
        "rotation": jnp.clip(jax.random.uniform(key_list[3], (N, H), jnp.float32, -3.140625, 3.140625), -3.140625, 3.140625),
        "readout": gaussian(key_list[4], (2, N, H), 0.25, 1.5, (), jnp.float32),
        "skip_gain": gaussian(key_list[5], (H,), 1.0, 4.0, (), jnp.float32),
        "projection": gaussian(key_list[6], (H, H), H ** -0.5, 0.375),
    }


PRECISE = lax.Precision.HIGHEST

def contract(form, table, data):
    return jnp.einsum(form, table, data, precision=PRECISE)

def complex_mul(left_re, left_im, right_re, right_im):
    return (left_re * right_re - left_im * right_im, left_re * right_im + left_im * right_re)

def powers(decay_rate, rotation, block_len):
    exponents = jnp.arange(block_len + 1).astype(jnp.float32)[:, None, None]
    magnitude = jnp.exp(-decay_rate[None] * exponents)
    return (magnitude * jnp.cos(rotation[None] * exponents), magnitude * jnp.sin(rotation[None] * exponents))

def kernels(pow_re, pow_im, readout, in_gain, block_len):
    kernel = lax.optimization_barrier(jnp.sum(in_gain * (readout[0] * pow_re[:block_len] - readout[1] * pow_im[:block_len]), axis=1))
    positions = jnp.arange(block_len)
    lag_index = positions[:, None] - positions[None, :]
    toeplitz = jnp.where((lag_index >= 0)[:, :, None], kernel[jnp.clip(lag_index, 0, block_len - 1)], 0.0)
    diag_table = (lag_index[:, :, None] == positions[None, None, :]).astype(jnp.float32)
    return (toeplitz, diag_table)

def reference(inputs, cotangent, decay_rate, rotation, readout, skip_gain, projection):
    clip_count, length, channels = inputs.shape
    block_len = BLOCK
    blocks = length // block_len
    pow_re, pow_im = powers(decay_rate, rotation, block_len)
    in_gain = jnp.sqrt(-jnp.expm1(-2.0 * decay_rate))
    toeplitz, diag_table = kernels(pow_re, pow_im, readout, in_gain, block_len)
    step_re, step_im = (pow_re[block_len], pow_im[block_len])
    segments = inputs.astype(jnp.float32).reshape(clip_count, blocks, block_len, channels).transpose(1, 0, 2, 3)

    def forward(carried, segment):
        state_re, state_im = carried
        mixed_re, mixed_im = complex_mul(readout[0], readout[1], state_re, state_im)
        within = contract('jnh,cnh->cjh', pow_re[1:], mixed_re) - contract('jnh,cnh->cjh', pow_im[1:], mixed_im)
        within = within + contract('jsh,csh->cjh', toeplitz, segment) + skip_gain * segment
        fill_re = in_gain * contract('snh,csh->cnh', pow_re[block_len - 1::-1], segment)
        fill_im = in_gain * contract('snh,csh->cnh', pow_im[block_len - 1::-1], segment)
        new_re, new_im = complex_mul(step_re, step_im, state_re, state_im)
        return ((new_re + fill_re, new_im + fill_im), within)
    zeros_state = jnp.zeros((clip_count,) + decay_rate.shape, jnp.float32)
    _, mixed_out = lax.scan(forward, (zeros_state, zeros_state), segments)
    mixed_out = mixed_out.transpose(1, 0, 2, 3).reshape(clip_count * length, channels)
    hidden = jax.nn.gelu(mixed_out, approximate=True).astype(jnp.bfloat16)
    flat_in = inputs.reshape(clip_count * length, channels)
    outputs = (flat_in.astype(jnp.float32) + jnp.dot(hidden, projection, preferred_element_type=jnp.float32)).astype(jnp.bfloat16)
    flat_tan = cotangent.reshape(clip_count * length, channels)
    proj_part = jnp.dot(hidden.T, flat_tan, preferred_element_type=jnp.float32)
    hidden_back = jnp.dot(flat_tan, projection.T, preferred_element_type=jnp.float32)
    _, gelu_back = jax.vjp(partial(jax.nn.gelu, approximate=True), mixed_out)
    mixed_grad = gelu_back(hidden_back)[0]
    grad_segments = mixed_grad.reshape(clip_count, blocks, block_len, channels).transpose(1, 0, 2, 3)

    def backward(carried, paired):
        next_re, next_im, acc_re, acc_im, correlation = carried
        grad_segment, segment = paired
        weighted_re, weighted_im = complex_mul(readout[0], readout[1], in_gain * next_re, in_gain * next_im)
        within = contract('snh,cnh->csh', pow_re[block_len:0:-1], weighted_re) - contract('snh,cnh->csh', pow_im[block_len:0:-1], weighted_im)
        within = within + contract('jsh,cjh->csh', toeplitz, grad_segment) + skip_gain * grad_segment
        lead_re = contract('snh,csh->cnh', pow_re[block_len:0:-1], segment)
        lead_im = contract('snh,csh->cnh', pow_im[block_len:0:-1], segment)
        prod_re, prod_im = complex_mul(lead_re, lead_im, next_re, next_im)
        acc_re = acc_re + in_gain * lax.optimization_barrier(jnp.sum(prod_re, axis=0))
        acc_im = acc_im + in_gain * lax.optimization_barrier(jnp.sum(prod_im, axis=0))
        correlation = correlation + contract('cjh,csh->jsh', grad_segment, segment)
        fresh_re = contract('jnh,cjh->cnh', pow_re[:block_len], grad_segment)
        fresh_im = contract('jnh,cjh->cnh', pow_im[:block_len], grad_segment)
        new_re, new_im = complex_mul(step_re, step_im, next_re, next_im)
        return ((new_re + fresh_re, new_im + fresh_im, acc_re, acc_im, correlation), within)
    zeros_acc = jnp.zeros(decay_rate.shape, jnp.float32)
    zeros_corr = jnp.zeros((block_len, block_len, channels), jnp.float32)
    carried, back_within = lax.scan(backward, (zeros_state, zeros_state, zeros_acc, zeros_acc, zeros_corr), (grad_segments, segments), reverse=True)
    acc_re, acc_im, correlation = (carried[2], carried[3], carried[4])
    back_within = back_within.transpose(1, 0, 2, 3).reshape(clip_count * length, channels)
    input_grad = (back_within + flat_tan.astype(jnp.float32)).reshape(clip_count, length, channels).astype(jnp.bfloat16)
    lag_sum = jnp.einsum('jsh,jsd->dh', correlation, diag_table, precision=PRECISE)
    acc_re = acc_re + in_gain * jnp.einsum('dnh,dh->nh', pow_re[:block_len], lag_sum, precision=PRECISE)
    acc_im = acc_im + in_gain * jnp.einsum('dnh,dh->nh', pow_im[:block_len], lag_sum, precision=PRECISE)
    readout_part = jnp.stack([acc_re, -acc_im])
    skip_part = lax.optimization_barrier(jnp.sum(mixed_grad * flat_in.astype(jnp.float32), axis=0))
    squares = jnp.sum(proj_part * proj_part) + jnp.sum(readout_part * readout_part) + jnp.sum(skip_part * skip_part)
    params = channels * channels + 2 * decay_rate.shape[0] * channels + channels
    ceiling = math.sqrt(params)
    factor = jnp.minimum(1.0, ceiling / (jnp.sqrt(squares) + 1e-06))
    return (outputs.reshape(clip_count, length, channels), input_grad, factor * proj_part, factor * readout_part, factor * skip_part)
```

```python
import math

import jax
import jax.numpy as jnp
from jax import lax
from jax.experimental import pallas as pl
from jax.experimental.pallas import tpu as pltpu
from jax.sharding import PartitionSpec as P

F32 = jnp.float32
TILE = 8
HALF = 128
GELU = math.sqrt(2.0 / math.pi)


def cmul(ar, ai, br, bi):
    return (ar * br - ai * bi, ar * bi + ai * br)


def call(body, out, *args, scratch=(), anywhere=False, flops=1_000_000):
    specs = {"in_specs": [pl.BlockSpec(memory_space=pl.ANY)] * len(args)} if anywhere else {}
    return pl.pallas_call(
        body,
        out_shape=out,
        **specs,
        scratch_shapes=list(scratch),
        compiler_params=pltpu.CompilerParams(vmem_limit_bytes=24 * 2**20),
        cost_estimate=pl.CostEstimate(flops=flops, bytes_accessed=500_000, transcendentals=0),
    )(*args)


def shape(*dims, dtype=F32):
    return jax.ShapeDtypeStruct(dims, dtype)


def gather_rows(parts):
    row = lax.broadcasted_iota(jnp.int32, parts[0].shape, 0)
    for bit in (1, 2, 4):
        mask = (row & bit) == 0
        parts = [
            jnp.where(mask, a, b) + pltpu.roll(jnp.where(mask, b, a), bit, 0)
            for a, b in zip(parts[::2], parts[1::2])
        ]
    return parts[0]


def states_sum(value):
    return jnp.sum(value.reshape(-1, TILE, value.shape[-1]), axis=0)


def end_state_kernel(u_any, decay_any, rotation_any, end_ref, lam_ref, u_in, decay, rotation, uf, sems):
    copies = [
        pltpu.make_async_copy(source, target, sems.at[i])
        for i, (source, target) in enumerate(
            ((decay_any, decay), (rotation_any, rotation), (u_any, u_in))
        )
    ]
    for copy in copies:
        copy.start()
    for copy in copies:
        copy.wait()
    magnitude = jnp.exp(-decay[...])
    lr = magnitude * jnp.cos(rotation[...])
    li = magnitude * jnp.sin(rotation[...])
    lam_ref[0] = lr
    lam_ref[1] = li
    uf[...] = u_in[0].astype(F32)
    length = uf.shape[0]

    def tile(k, carried):
        re, im = carried
        rows = uf[pl.ds(pl.multiple_of(k * TILE, TILE), TILE), :]
        for j in range(TILE):
            re, im = (lr * re - li * im + rows[j : j + 1], lr * im + li * re)
        return re, im

    zero = jnp.zeros_like(lr)
    re, im = lax.fori_loop(0, length // TILE, tile, (zero, zero))
    to_pieces(end_ref, re, im)


def to_pieces(pieces, re, im):
    rows = pieces.shape[1] // 2
    halves = re.shape[1] // HALF
    for p in range(pieces.shape[0]):
        first, lane = (p // halves) * rows, (p % halves) * HALF
        pieces[p, :rows, :] = re[first : first + rows, lane : lane + HALF]
        pieces[p, rows:, :] = im[first : first + rows, lane : lane + HALF]


def from_pieces(pieces, state):
    rows = pieces.shape[1] // 2
    halves = state.shape[2] // HALF
    for p in range(pieces.shape[0]):
        first, lane = (p // halves) * rows, (p % halves) * HALF
        for kind in (0, 1):
            state[kind, pl.ds(first, rows), pl.ds(lane, HALF)] = pieces[
                p, pl.ds(kind * rows, rows), :
            ]


def side_kernel(length, lam_ref, cot_ref, proj_ref, hb_ref, span_ref):
    hb_ref[...] = lax.dot_general(
        cot_ref[0], proj_ref[...], (((1,), (1,)), ((), ())), preferred_element_type=F32
    )
    base = (lam_ref[0], lam_ref[1])
    span = None
    exponent = length
    while exponent:
        if exponent & 1:
            span = base if span is None else cmul(*span, *base)
        exponent >>= 1
        if exponent:
            base = cmul(*base, *base)
    to_pieces(span_ref, *span)


def prefix_kernel(backward, got_ref, span_ref, out_ref):
    count = got_ref.shape[0]
    rows = got_ref.shape[1] // 2
    upper, lower = pl.ds(0, rows), pl.ds(rows, rows)
    mine = lax.axis_index("seq")
    sr, si = span_ref[mine, upper, :], span_ref[mine, lower, :]
    re, im = jnp.zeros_like(sr), jnp.zeros_like(si)
    order = range(count)
    for place in reversed(order) if backward else order:
        out_ref[place, upper, :] = re
        out_ref[place, lower, :] = im
        re, im = cmul(sr, si, re, im)
        re, im = re + got_ref[place, upper, :], im + got_ref[place, lower, :]


def carry(value, span, backward):
    got = lax.all_to_all(value, "seq", 0, 0, tiled=True)

    def body(*refs):
        prefix_kernel(backward, *refs)

    out = call(body, shape(*value.shape), got, span)
    return lax.all_to_all(out, "seq", 0, 0, tiled=True)


def middle_kernel(*refs):
    got_ref, u_ref, cot_ref, hb_ref, lam_ref, gain_ref, readout_ref, skip_ref = refs[:8]
    start_ref, hidden_ref, m_ref, stage = refs[8:12]
    uf, mixed, enter, start = refs[12:]
    length, channels = uf.shape
    tiles = length // TILE
    half_rows = stage.shape[0] // (channels // HALF)
    uf[...] = u_ref[0].astype(F32)
    from_pieces(got_ref, enter)

    for lane in range(0, channels, HALF):
        cols = pl.ds(lane, HALF)
        lr, li = lam_ref[0, :, cols], lam_ref[1, :, cols]
        cr = gain_ref[:, cols] * readout_ref[0, :, cols]
        ci = gain_ref[:, cols] * readout_ref[1, :, cols]

        def forward(k, carried):
            re, im = carried
            here = pl.ds(pl.multiple_of(k * TILE, TILE), TILE)
            rows = uf[here, cols]
            parts = []
            for j in range(TILE):
                re, im = (lr * re - li * im + rows[j : j + 1], lr * im + li * re)
                parts.append(states_sum(cr * re - ci * im))
            mixed[here, cols] = gather_rows(parts)
            return re, im

        lax.fori_loop(0, tiles, forward, (enter[0, :, cols], enter[1, :, cols]))

    x = mixed[...] + skip_ref[...] * uf[...]
    square = x * x
    t = jnp.tanh(GELU * x * (1.0 + 0.044715 * square))
    hidden = (0.5 * x * (1.0 + t)).astype(jnp.bfloat16)
    hidden_ref[...] = hidden
    slope = 0.5 * (1.0 + t) + 0.5 * x * (1.0 - t * t) * (GELU * (1.0 + 3 * 0.044715 * square))
    m = hb_ref[...] * slope
    m_ref[...] = m
    states = lam_ref.shape[1]
    used = channels + 2 * states
    skip_part = jnp.sum(m * uf[...], axis=0, keepdims=True)
    proj_part = lax.dot_general(
        hidden, cot_ref[0], (((0,), (0,)), ((), ())), preferred_element_type=F32
    )
    for half in range(channels // HALF):
        first, lane = half * half_rows, half * HALF
        stage[pl.ds(first + used, half_rows - used), :] = jnp.zeros((half_rows - used, HALF), F32)
        stage[pl.ds(first + used, 1), :] = skip_part[:, lane : lane + HALF]
        stage[pl.ds(first, channels), :] = proj_part[:, lane : lane + HALF]

    for lane in range(0, channels, HALF):
        cols = pl.ds(lane, HALF)
        lr, li = lam_ref[0, :, cols], lam_ref[1, :, cols]

        def back(k, carried):
            re, im, gr, gi = carried
            here = pl.ds(pl.multiple_of((tiles - 1 - k) * TILE, TILE), TILE)
            rows = m_ref[here, cols]
            samples = uf[here, cols]
            for j in reversed(range(TILE)):
                re, im = (lr * re - li * im + rows[j : j + 1], lr * im + li * re)
                gr, gi = (gr + samples[j : j + 1] * re, gi + samples[j : j + 1] * im)
            return re, im, gr, gi

        zero = jnp.zeros_like(lr)
        re, im, gr, gi = lax.fori_loop(0, tiles, back, (zero,) * 4)
        start[0, :, cols] = re
        start[1, :, cols] = im
        er, ei = cmul(lr, li, enter[0, :, cols], enter[1, :, cols])
        er, ei = cmul(er, ei, re, im)
        gain = gain_ref[:, cols]
        first = (lane // HALF) * half_rows + channels
        stage[pl.ds(first, states), :] = gain * (gr + er)
        stage[pl.ds(first + states, states), :] = -gain * (gi + ei)

    to_pieces(start_ref, start[0], start[1])


def outputs_kernel(u_ref, hidden_ref, proj_ref, out_ref):
    product = jnp.dot(hidden_ref[...], proj_ref[...], preferred_element_type=F32)
    out_ref[0] = (u_ref[0].astype(F32) + product).astype(jnp.bfloat16)


def input_grad_kernel(*refs):
    got_ref, m_ref, cot_ref, lam_ref, gain_ref, readout_ref, skip_ref, out_ref, grad, leave = refs
    length, channels = m_ref.shape
    tiles = length // TILE
    from_pieces(got_ref, leave)

    for lane in range(0, channels, HALF):
        cols = pl.ds(lane, HALF)
        lr, li = lam_ref[0, :, cols], lam_ref[1, :, cols]
        cr = gain_ref[:, cols] * readout_ref[0, :, cols]
        ci = gain_ref[:, cols] * readout_ref[1, :, cols]

        def back(k, carried):
            re, im = carried
            here = pl.ds(pl.multiple_of((tiles - 1 - k) * TILE, TILE), TILE)
            rows = m_ref[here, cols]
            parts = [None] * TILE
            for j in reversed(range(TILE)):
                re, im = (lr * re - li * im + rows[j : j + 1], lr * im + li * re)
                parts[j] = states_sum(cr * re - ci * im)
            grad[here, cols] = gather_rows(parts)
            return re, im

        lax.fori_loop(0, tiles, back, (leave[0, :, cols], leave[1, :, cols]))

    total = grad[...] + skip_ref[...] * m_ref[...] + cot_ref[0].astype(F32)
    out_ref[0] = total.astype(jnp.bfloat16)


def sum_kernel(devices, got_ref, out_ref):
    chunk = got_ref.shape[0] // devices
    total = got_ref[pl.ds(0, chunk), :]
    for i in range(1, devices):
        total = total + got_ref[pl.ds(i * chunk, chunk), :]
    for i in range(devices):
        out_ref[pl.ds(i * chunk, chunk), :] = total


def clip_kernel(got_ref, proj_ref, readout_ref, skip_ref):
    channels = proj_ref.shape[0]
    states = readout_ref.shape[1]
    halves = channels // HALF
    half_rows = got_ref.shape[0] // halves
    ceiling = math.sqrt(channels * channels + 2 * states * channels + channels)
    values = got_ref[...]
    norm = jnp.sqrt(jnp.full((1, HALF), jnp.sum(values * values), F32))
    factor = jnp.minimum(1.0, ceiling / (norm + 1e-06))
    for half in range(halves):
        first, cols = half * half_rows, pl.ds(half * HALF, HALF)
        proj_ref[:, cols] = factor * got_ref[pl.ds(first, channels), :]
        first += channels
        readout_ref[0, :, cols] = factor * got_ref[pl.ds(first, states), :]
        readout_ref[1, :, cols] = factor * got_ref[pl.ds(first + states, states), :]
        skip_ref[:, cols] = factor * got_ref[pl.ds(first + 2 * states, 1), :]


def shards(inputs, cotangent, decay_rate, rotation, readout, skip_gain, projection):
    length, channels = inputs.shape[1:]
    states = decay_rate.shape[0]
    count = lax.axis_size("seq")
    devices = count * lax.axis_size("batch")
    halves = channels // HALF
    skip = skip_gain.reshape(1, channels)
    state = shape(2, states, channels)
    piece_rows = 2 * states * halves // count
    assert piece_rows * count == 2 * states * halves and piece_rows % 2 == 0
    pieces = shape(count, piece_rows, HALF)
    plane = (length, channels)
    with jax.named_scope("end_state"):
        end, lam = call(
            end_state_kernel,
            (pieces, state),
            inputs,
            decay_rate,
            rotation,
            anywhere=True,
            scratch=[
                pltpu.VMEM((1, *plane), jnp.bfloat16),
                pltpu.VMEM((states, channels), F32),
                pltpu.VMEM((states, channels), F32),
                pltpu.VMEM(plane, F32),
                pltpu.SemaphoreType.DMA((3,)),
            ],
        )
    gain = jnp.sqrt(-jnp.expm1(-2.0 * decay_rate))

    def side_body(*refs):
        side_kernel(length, *refs)

    with jax.named_scope("side"):
        hb, span = call(side_body, (shape(*plane), pieces), lam, cotangent, projection)
    with jax.named_scope("forward_carry"):
        enter = carry(end, span, False)
    rows = channels + 2 * states + 1
    chunk = -(-rows * halves // (devices * TILE)) * TILE

    with jax.named_scope("middle"):
        start, hidden, m, parts = call(
            middle_kernel,
            (
                pieces,
                shape(*plane, dtype=jnp.bfloat16),
                shape(*plane),
                shape(devices * chunk, HALF),
            ),
            enter,
            inputs,
            cotangent,
            hb,
            lam,
            gain,
            readout,
            skip,
            scratch=[
                pltpu.VMEM(plane, F32),
                pltpu.VMEM(plane, F32),
                pltpu.VMEM((2, states, channels), F32),
                pltpu.VMEM((2, states, channels), F32),
            ],
        )
    with jax.named_scope("adjoint_carry"):
        leave = carry(start, span, True)

    def sum_body(*refs):
        sum_kernel(devices, *refs)

    with jax.named_scope("gradient_sum"):
        got = lax.all_to_all(parts, ("seq", "batch"), 0, 0, tiled=True)
        total = call(sum_body, shape(*parts.shape), got)
        total = lax.all_to_all(total, ("seq", "batch"), 0, 0, tiled=True)
    with jax.named_scope("layer_outputs"):
        outputs = call(
            outputs_kernel, shape(1, *plane, dtype=jnp.bfloat16), inputs, hidden, projection
        )
    with jax.named_scope("input_grad"):
        input_grad = call(
            input_grad_kernel,
            shape(1, *plane, dtype=jnp.bfloat16),
            leave,
            m,
            cotangent,
            lam,
            gain,
            readout,
            skip,
            scratch=[pltpu.VMEM(plane, F32), pltpu.VMEM((2, states, channels), F32)],
        )
    with jax.named_scope("clip"):
        proj_grad, readout_grad, skip_grad = call(
            clip_kernel, (shape(channels, channels), state, shape(1, channels)), total
        )
    return (outputs, input_grad, proj_grad, readout_grad, skip_grad.reshape(channels))


def solution(mesh):
    placed = (P("batch", "seq", None), P("batch", "seq", None), P(), P(), P(), P(), P())
    return jax.shard_map(
        shards,
        mesh=mesh,
        in_specs=placed,
        out_specs=(P("batch", "seq", None), P("batch", "seq", None), P(), P(), P()),
        check_vma=False,
    )
```
